32 devices in a mesh: cuts: 4 (over y, core), mode: 8 (over z, x).
Axes of the slice: x: 2, y: 2, z: 4, core: 2. Of those that a mesh axis runs over, the one named last changes fastest.
Arguments:
- stem: bfloat16 [4, 2, 1024, 1024], P('cuts', None, None, 'mode'), may hold values from -6 to 6
- branches: bfloat16 [3, 2, 1024, 1024], P(None, None, None, 'mode'), may hold values from -0.125 to 0.125
- order: int32 [3], replicated, may hold values from 0 to 2, each once
- swap_order: int32 [3, 1024], replicated, may hold values from 0 to 1023, each once within a row
- row_bits: int32 [2048], replicated, may hold values from 0 to 1023
- column_bits: int32 [2048], replicated, may hold values from 0 to 1023
Outputs:
- stem_out: bfloat16 [4, 2, 1024, 1024], P('cuts', None, None, 'mode')
- amplitudes: float32 [2, 2048], P(None, ('cuts', 'mode'))
The draws below stay inside these ranges and needn't reach their ends.
All inputs are finite; a program needn't handle non-finite values.
Results may differ from the reference program's by a relative error of at most 0.009.
Values may be sent and summed in bfloat16 or wider, within the bound.
No kernel may reach another device: no remote copies, remote signals or barrier semaphores. Data moves between devices by JAX's collectives and lax.ppermute only.
A program may use at most 128 MiB of HBM per device.

```python
import jax
import jax.numpy as jnp
from jax import lax

K = 1024
STEPS = 3
NB = 2048
SLICES = 4
COLS = 1024
N_MODE = 8


def touch_ends(array, rng, smallest, high):
    longest = array.shape.index(max(array.shape))
    spots = []
    for shift in (0, 1):
        where = [jax.random.randint(jax.random.fold_in(rng, axis), (), 0, length) for axis, length in enumerate(array.shape)]
        where[longest] = (where[longest] + shift) % array.shape[longest]
        spots.append(tuple(where))
    return array.at[spots[0]].set(smallest).at[spots[1]].set(high)


def levels(key, shape, cuts, smallest, largest):
    factor_of, own = 1.0, jax.random.fold_in(key, 6)
    for dim, shards_of in cuts:
        draws = jnp.exp(jax.random.uniform(jax.random.fold_in(own, dim), (shards_of,), jnp.float32, smallest / len(cuts), largest / len(cuts)))
        factor_of = factor_of * jnp.repeat(draws, shape[dim] // shards_of).reshape([-1 if axis == dim else 1 for axis in range(len(shape))])
    return factor_of


def gaussian(key, dims, scale, bound, cuts=(), held_as=jnp.bfloat16):
    array = jax.random.normal(key, dims, jnp.float32) * scale
    if len(cuts) > 0:
        array = levels(key, dims, cuts, -0.22, 0.18) * array
    return jnp.clip(array, min=-bound, max=bound).astype(held_as)


def setup_inputs(seed: int = 0) -> dict:
    key_list = jax.random.split(jax.random.key(seed), 7)
    stem = gaussian(key_list[0], (SLICES, 2, K, COLS), 1.0, 6.0, ((0, 4), (3, 8)))
    branches = gaussian(key_list[1], (STEPS, 2, K, K), (2 * K) ** -0.5, 0.125, ((3, 8),))
    order = jax.random.permutation(key_list[2], STEPS).astype(jnp.int32)
    swap_order = jax.vmap(lambda own: jax.random.permutation(own, K))(jax.random.split(key_list[3], STEPS)).reshape((STEPS, K)).astype(jnp.int32)
    row_bits = touch_ends(jax.random.randint(key_list[4], (NB,), 0, K), jax.random.fold_in(key_list[4], 1), 0, K - 1).astype(jnp.int32)
    column_bits = touch_ends(jax.random.randint(key_list[5], (NB,), 0, COLS), jax.random.fold_in(key_list[5], 1), 0, COLS - 1).astype(jnp.int32)
    return {"stem": stem, "branches": branches, "order": order, "swap_order": swap_order, "row_bits": row_bits, "column_bits": column_bits}


def swap_modes(field, groups):
    slices, two, width, cols = field.shape
    rows = cols // groups
    view = field.reshape(slices, two, groups, width // groups, groups, rows)
    view = view.transpose(0, 1, 4, 3, 2, 5)
    return view.reshape(slices, two, width, cols)


def absorb_slice(matrix, part):
    first = matrix[0]
    second = matrix[1]
    xreal = part[0].astype(jnp.float32)
    ximag = part[1].astype(jnp.float32)
    hp = lax.Precision.HIGHEST
    real = jnp.einsum("io,ic->oc", first, xreal, precision=hp) - jnp.einsum("io,ic->oc", second, ximag, precision=hp)
    imag = jnp.einsum("io,ic->oc", first, ximag, precision=hp) + jnp.einsum("io,ic->oc", second, xreal, precision=hp)
    return jnp.stack([real, imag], axis=0).astype(jnp.bfloat16)


def reference(stem, branches, order, swap_order, row_bits, column_bits):
    field = stem
    for step in range(STEPS):
        field = jnp.take(field, swap_order[step].astype(jnp.int32), axis=2)
        field = swap_modes(field, N_MODE)
        matrix = lax.dynamic_index_in_dim(branches, order[step].astype(jnp.int32), 0, keepdims=False).astype(jnp.float32)
        field = lax.map(lambda part: absorb_slice(matrix, part), field)
    picked = field[:, :, row_bits, column_bits].astype(jnp.float32)
    amplitudes = jnp.sum(picked, axis=0)
    return field, amplitudes
```

```python
import functools

import jax
import jax.numpy as jnp
from jax import lax
from jax.experimental import pallas as pl
from jax.experimental.pallas import tpu as pltpu
from jax.sharding import PartitionSpec as P

EVERY = ("cuts", "mode")
ROOM = 48 * 2**20


def vmem(count):
    return [pl.BlockSpec(memory_space=pltpu.VMEM)] * count


def one_hot(places, first, length):
    states = first + lax.broadcasted_iota(jnp.int32, (length, places.shape[1]), 0)
    return jnp.where(states == places, 1.0, 0.0).astype(jnp.bfloat16)


def dot(left, right, over_left=1):
    return lax.dot_general(left, right, (((over_left,), (0,)), ((), ())), preferred_element_type=jnp.float32)


def chunks_of(width):
    size = 256 if width % 256 == 0 else width
    return [slice(start, start + size) for start in range(0, width, size)]


def spread_kernel(stem, places, out):
    groups, _, block, width = out.shape
    for cut in chunks_of(width):
        choose = one_hot(places[:, cut], 0, width)
        for part in range(2):
            moved = dot(stem[part], choose, 0).astype(jnp.bfloat16)
            for m in range(groups):
                out[m, part, :, cut] = moved[m * block : (m + 1) * block]


def spread(stem, places, groups):
    _, width, rows = stem.shape
    return pl.pallas_call(
        spread_kernel,
        out_shape=jax.ShapeDtypeStruct((groups, 2, rows // groups, width), stem.dtype),
        in_specs=vmem(2),
        out_specs=vmem(1)[0],
        compiler_params=pltpu.CompilerParams(vmem_limit_bytes=ROOM),
    )(stem, places)


def step_kernel(plan, last, *refs):
    pick, field, places = refs[:3]
    pieces, (out, matrix, packed, semaphore) = refs[3:-4], refs[-4:]
    groups, _, block, width = field.shape
    low = width // groups
    rows = groups * block
    copies = [
        pltpu.make_async_copy(source(pieces, pick), matrix.at[where], semaphore.at[number])
        for number, (source, where) in enumerate(plan)
    ]
    for copy in copies:
        copy.start()
    for a in range(groups):
        for b in range(groups):
            real = field[a, 0, :, b * low : (b + 1) * low]
            imag = field[a, 1, :, b * low : (b + 1) * low]
            at, to = slice(b * block, (b + 1) * block), slice(a * low, (a + 1) * low)
            after = slice(width + a * low, width + (a + 1) * low)
            packed[at, to] = real
            packed[at, after] = -imag
            packed[rows + b * block : rows + (b + 1) * block, to] = imag
            packed[rows + b * block : rows + (b + 1) * block, after] = real
    for copy in copies:
        copy.wait()
    whole = []
    for cut in chunks_of(width):
        side = matrix[:, :, cut].reshape(2 * width, cut.stop - cut.start)
        whole.append(dot(packed[...], side).astype(jnp.bfloat16))
    result = jnp.concatenate(whole, axis=1)
    if last:
        for part in range(2):
            for c in range(groups):
                start = part * rows + c * block
                out[c, part] = result[start : start + block]
        return
    for cut in chunks_of(width):
        moved = dot(result, one_hot(places[:, cut], 0, width)).astype(jnp.bfloat16)
        for part in range(2):
            for c in range(groups):
                start = part * rows + c * block
                out[c, part, :, cut] = moved[start : start + block]


def step_of(plan, last, pick, field, places, pieces):
    groups, _, block, width = field.shape
    return pl.pallas_call(
        functools.partial(step_kernel, plan, last),
        out_shape=jax.ShapeDtypeStruct(field.shape, field.dtype),
        in_specs=[pl.BlockSpec(memory_space=pltpu.SMEM), *vmem(2)] + [pl.BlockSpec(memory_space=pl.ANY)] * len(pieces),
        out_specs=vmem(1)[0],
        scratch_shapes=[
            pltpu.VMEM((2, width, width), field.dtype),
            pltpu.VMEM((2 * groups * block, 2 * width), field.dtype),
            pltpu.SemaphoreType.DMA((len(plan),)),
        ],
        compiler_params=pltpu.CompilerParams(vmem_limit_bytes=ROOM),
    )(pick, field, places, *pieces)


def pick_kernel(field, states, spots, out):
    groups, _, block, width = field.shape
    rows = groups * block
    whole = jnp.concatenate([field[:, part].reshape(rows, width) for part in range(2)], axis=0)
    for cut in chunks_of(states.shape[1]):
        found = dot(whole, one_hot(states[:, cut], 0, width))
        here = lax.broadcasted_iota(jnp.int32, (rows, cut.stop - cut.start), 0) == spots[:, cut]
        for part in range(2):
            value = jnp.where(here, found[part * rows : (part + 1) * rows], 0.0)
            out[part : part + 1, cut] = jnp.sum(value, axis=0, keepdims=True)


def pick_entries(field, states, spots):
    return pl.pallas_call(
        pick_kernel,
        out_shape=jax.ShapeDtypeStruct((2, states.shape[1]), jnp.float32),
        in_specs=vmem(3),
        out_specs=vmem(1)[0],
        compiler_params=pltpu.CompilerParams(vmem_limit_bytes=ROOM),
    )(field, states, spots)


def collect_kernel(field, out):
    groups, _, block, width = field.shape
    for part in range(2):
        rows = field[:, part].reshape(groups * block, width)
        out[part] = jnp.transpose(rows)


def collect(field):
    groups, _, block, width = field.shape
    return pl.pallas_call(
        collect_kernel,
        out_shape=jax.ShapeDtypeStruct((2, width, groups * block), field.dtype),
        in_specs=vmem(1),
        out_specs=vmem(1)[0],
        compiler_params=pltpu.CompilerParams(vmem_limit_bytes=ROOM),
    )(field)


def add_up(values):
    devices = lax.axis_size(EVERY)
    share = values.shape[1] // devices
    blocks = values.reshape(2, devices, share).transpose(1, 0, 2)
    return jnp.sum(lax.all_to_all(blocks, EVERY, 0, 0), axis=0)


def batched(stem, branches, order, swap_order, row_bits, column_bits):
    local = stem[0]
    groups = lax.axis_size("mode")
    cuts = lax.axis_size("cuts")
    _, width, rows = local.shape
    block = rows // groups
    steps = swap_order.shape[0]
    places = [swap_order[step][None] for step in range(steps)]
    part = width // cuts
    own = lax.dynamic_slice_in_dim(branches, lax.axis_index("cuts") * part, part, 2)
    gathered = lax.all_gather(own, EVERY, axis=0)
    field = lax.all_to_all(spread(local, places[0], groups), "mode", 0, 0)
    plan = []
    for c in range(cuts):
        for g in range(groups):
            where = (slice(None), pl.ds(c * part, part), pl.ds(g * rows, rows))
            plan.append((lambda pieces, pick, at=c * groups + g: pieces[0].at[at, pick[0]], where))
    for step in range(steps):
        last = step == steps - 1
        field = step_of(plan, last, order[step][None], field, places[0 if last else step + 1], [gathered])
    low = column_bits % rows - lax.axis_index("mode") * block
    inside = jnp.logical_and(low >= 0, low < block)
    spots = jnp.where(inside, column_bits // rows * block + low, -1)
    values = pick_entries(field, row_bits[None], spots[None])
    result = collect(lax.all_to_all(field, "mode", 0, 0))
    return result[None], add_up(values)


def stepwise(stem, branches, order, swap_order, row_bits, column_bits):
    local = stem[0]
    groups = lax.axis_size("mode")
    _, width, rows = local.shape
    states = jnp.arange(width)[:, None]

    def product(left, right):
        return lax.dot_general(left, right, (((0,), (0,)), ((), ())), preferred_element_type=jnp.float32)

    for step in range(swap_order.shape[0]):
        choose = (states == swap_order[step][None]).astype(local.dtype)
        moved = jnp.stack([product(choose, local[part]).astype(local.dtype) for part in range(2)])
        view = moved.reshape(2, groups, width // groups, rows)
        swapped = lax.all_to_all(view, "mode", split_axis=1, concat_axis=1, tiled=True)
        field = swapped.reshape(2, width, rows)
        shard = lax.dynamic_index_in_dim(branches, order[step], 0, keepdims=False)
        matrix = lax.all_gather(shard, "mode", axis=2, tiled=True)
        real = product(matrix[0], field[0]) - product(matrix[1], field[1])
        imag = product(matrix[0], field[1]) + product(matrix[1], field[0])
        local = jnp.stack([real, imag]).astype(local.dtype)
    chosen = (states == row_bits[None]).astype(local.dtype)
    column = column_bits - lax.axis_index("mode") * rows
    here = jnp.arange(rows)[:, None] == column[None]
    values = jnp.stack([jnp.sum(jnp.where(here, product(local[part], chosen), 0.0), axis=0) for part in range(2)])
    return local[None], add_up(values)


def solution(mesh):
    groups, cuts = mesh.shape["mode"], mesh.shape["cuts"]

    def body(stem, branches, *rest):
        _, _, width, rows = stem.shape
        fits = rows % (16 * groups) == 0 and width % (128 * groups) == 0 and branches.shape[3] == rows
        fits = fits and rows % 128 == 0 and width % (16 * cuts) == 0
        return (batched if fits else stepwise)(stem, branches, *rest)

    return jax.shard_map(
        body,
        mesh=mesh,
        in_specs=(P("cuts", None, None, "mode"), P(None, None, None, "mode"), P(), P(), P(), P()),
        out_specs=(P("cuts", None, None, "mode"), P(None, EVERY)),
        check_vma=False,
    )
```
